32 devices in a mesh: dof: 8 (over z, x), snap: 4 (over y, core).
Axes of the slice: x: 2, y: 2, z: 4, core: 2. Of those that a mesh axis runs over, the one named last changes fastest.
Arguments:
- snapshots: bfloat16 [32768, 1024], P('dof', 'snap')
- lengths: int32 [16], replicated, may hold values from 16 to 64, as said below
- start_block: float32 [1024, 128], replicated, may hold values from -6 to 6
Outputs:
- pod_modes: float32 [32768, 128], P(('dof', 'snap'))
- r_factor: float32 [1024, 1024], replicated
The draws below stay inside these ranges and needn't reach their ends.
Inputs may be any that keep to these rules, and one draw needn't show every extreme that they name: `lengths`: some passage has all 64 steps active and some passage only a quarter of them.
All inputs are finite; a program needn't handle non-finite values.
Results may differ from the reference program's by a relative error of at most 0.0003.
Values may be sent and summed in bfloat16 or wider, within the bound.
A program may use at most 128 MiB of HBM per device.

```python
import math
import jax
import jax.numpy as jnp
from jax import lax

NS = 1024
STEPS = 64
MODES = 128
ITERS = 3
PASSES = 16
M = 32768


def draw_snapshots(key, part):
    keys = jax.random.split(key, 3)
    row_scale = jnp.exp(jax.random.uniform(keys[0], (M, 1), jnp.float32, math.log(0.3), math.log(3.0)))
    col_scale = jnp.exp(jax.random.uniform(keys[1], (1, NS), jnp.float32, math.log(0.3), math.log(3.0)))
    base = jax.random.normal(keys[2], (M, NS), jnp.float32)
    return (base * row_scale * col_scale).astype(jnp.bfloat16)


def draw_lengths(key, part):
    keys = jax.random.split(key, 2)
    values = jax.random.randint(keys[0], (PASSES,), STEPS // 4, STEPS + 1)
    order = jax.random.permutation(keys[1], PASSES)
    values = values.at[order[0]].set(STEPS)
    values = values.at[order[1]].set(STEPS // 4)
    return values.astype(jnp.int32)


def centred(rng, extent, scale, most, kind=jnp.bfloat16):
    return jnp.clip(scale * jax.random.normal(rng, extent, jnp.float32), -most, most).astype(kind)


def setup_inputs(seed: int = 0) -> dict:
    splits = jax.random.split(jax.random.key(seed), 4)
    return {
        "snapshots": draw_snapshots(jax.random.fold_in(splits[3], 71), 0),
        "lengths": draw_lengths(jax.random.fold_in(splits[3], 71), 0),
        "start_block": centred(splits[2], (NS, MODES), 1.0, 6.0, jnp.float32),
    }


def reference(snapshots, lengths, start_block):
    columns = jnp.arange(NS, dtype=jnp.int32)
    col_length = lengths[(columns // STEPS).astype(jnp.int32)]
    active = columns % STEPS < col_length
    masked = jnp.where(active[None, :], snapshots, jnp.zeros_like(snapshots))
    gram_sum = jnp.dot(masked.T.astype(jnp.float32), masked.astype(jnp.float32), preferred_element_type=jnp.float32)
    shifted = gram_sum / jnp.float32(M) + 0.05 * jnp.eye(NS, dtype=jnp.float32)
    upper_factor = jnp.linalg.cholesky(shifted).T
    subspace = start_block
    for sweep in range(ITERS):
        image = jnp.dot(shifted.astype(jnp.float32), subspace.astype(jnp.float32), precision=lax.Precision.HIGHEST, preferred_element_type=jnp.float32)
        correlation = jnp.dot(image.T.astype(jnp.float32), image.astype(jnp.float32), precision=lax.Precision.HIGHEST, preferred_element_type=jnp.float32)
        lower_factor = jnp.linalg.cholesky(correlation)
        subspace = lax.linalg.triangular_solve(lower_factor, image, left_side=False, lower=True, transpose_a=True)
    pod_modes = jnp.dot(masked.astype(jnp.float32), subspace.astype(jnp.float32), precision=lax.Precision.HIGHEST, preferred_element_type=jnp.float32)
    return (pod_modes, upper_factor)
```

```python
import functools

import jax
import jax.numpy as jnp
from jax import lax
from jax.experimental import pallas as pl
from jax.experimental.pallas import tpu as pltpu
from jax.sharding import PartitionSpec as P

STEPS = 64
ITERS = 3
PASSES = 16
B = 128
VMEM_LIMIT = 48 * 1024 * 1024
F32 = jnp.float32
BF16 = jnp.bfloat16
COL0 = (((0,), (0,)), ((), ()))
ROWCOL = (((1,), (0,)), ((), ()))
COLCOL = (((1,), (1,)), ((), ()))


def split3(x):
    hi = x.astype(BF16)
    rest = x - hi.astype(F32)
    mid = rest.astype(BF16)
    low = (rest - mid.astype(F32)).astype(BF16)
    return hi, mid, low


def dot6(a, b, dims):
    return lax.dot_general(
        a, b, dims, precision=lax.Precision.HIGHEST, preferred_element_type=F32
    )


def factor_block(block):
    rows = [None] * (B // 8)
    for i in range(B // 8):
        r = lax.broadcasted_iota(jnp.int32, (8, B), 0) + 8 * i
        c = lax.broadcasted_iota(jnp.int32, (8, B), 1)
        rows[i] = (block[8 * i : 8 * i + 8, :], jnp.where(r == c, 1.0, 0.0).astype(F32))
    sub = lax.broadcasted_iota(jnp.int32, (8, B), 0)
    upper, inverse = [], []
    for g in range(B // 8):
        left, right = rows[g]
        cols = [
            jnp.broadcast_to(left[:, 8 * g + t : 8 * g + t + 1], (8, B)) for t in range(8)
        ]
        outer = [
            [
                jnp.broadcast_to(rows[i][0][:, 8 * g + t : 8 * g + t + 1], (8, B))
                for t in range(8)
            ]
            for i in range(g + 1, B // 8)
        ]
        u_tile = jnp.zeros((8, B), F32)
        v_tile = jnp.zeros((8, B), F32)
        for t in range(8):
            pivot = jnp.broadcast_to(cols[t][t : t + 1, :], (8, B))
            recip = 1.0 / pivot
            scale = lax.rsqrt(pivot)
            left_row = jnp.broadcast_to(left[t : t + 1, :], (8, B))
            right_row = jnp.broadcast_to(right[t : t + 1, :], (8, B))
            u_tile = jnp.where(sub == t, left_row * scale, u_tile)
            v_tile = jnp.where(sub == t, right_row * scale, v_tile)
            factor = jnp.where(sub == t, cols[t] - 1.0, cols[t]) * recip
            left_new = jnp.where(sub == t, left_row * recip, left - factor * left_row)
            right_new = jnp.where(sub == t, right_row * recip, right - factor * right_row)
            for c in range(t + 1, 8):
                head = jnp.broadcast_to(cols[c][t : t + 1, :], (8, B))
                cols[c] = jnp.where(sub == t, head * recip, cols[c] - factor * head)
            left, right = left_new, right_new
        upper.append(u_tile)
        inverse.append(v_tile)
        left_rows = [jnp.broadcast_to(left[t : t + 1, :], (8, B)) for t in range(8)]
        right_rows = [jnp.broadcast_to(right[t : t + 1, :], (8, B)) for t in range(8)]
        for i in range(g + 1, B // 8):
            a, b = rows[i]
            coef = outer[i - g - 1]
            for t in range(8):
                a = a - coef[t] * left_rows[t]
                b = b - coef[t] * right_rows[t]
            rows[i] = (a, b)
    u = jnp.concatenate(upper, axis=0)
    v = jnp.concatenate(inverse, axis=0)
    r = lax.broadcasted_iota(jnp.int32, (B, B), 0)
    c = lax.broadcasted_iota(jnp.int32, (B, B), 1)
    return jnp.where(c >= r, u, 0.0), v


def cholesky_kernel(a_ref, r_ref, left_ref, right_ref, diag_ref, inv_ref):
    width = a_ref.shape[0]
    count = width // B
    r_ref[...] = a_ref[...]

    @pl.loop(0, count)
    def panel(k):
        here = pl.ds(pl.multiple_of(k * B, B), B)
        u, v = factor_block(r_ref[here, here])
        row = dot6(v, r_ref[here, :], ROWCOL)
        col = lax.broadcasted_iota(jnp.int32, (B, width), 1)
        row = jnp.where(col >= (k + 1) * B, row, 0.0)
        r_ref[here, :] = row
        r_ref[here, here] = u
        hi, mid, low = split3(row)
        left_ref[...] = jnp.concatenate([hi, mid, hi, low, mid, hi], axis=0)
        right_ref[...] = jnp.concatenate([hi, hi, mid, hi, mid, low], axis=0)

        @pl.loop(k + 1, count)
        def update(i):
            there = pl.ds(pl.multiple_of(i * B, B), B)
            r_ref[there, :] = r_ref[there, :] - lax.dot_general(
                left_ref[:, there], right_ref[...], COL0, preferred_element_type=F32
            )


def cholesky(shifted):
    width = shifted.shape[0]
    return pl.pallas_call(
        cholesky_kernel,
        out_shape=jax.ShapeDtypeStruct((width, width), F32),
        in_specs=[pl.BlockSpec(memory_space=pltpu.VMEM)],
        out_specs=pl.BlockSpec(memory_space=pltpu.VMEM),
        scratch_shapes=[
            pltpu.VMEM((6 * B, width), BF16),
            pltpu.VMEM((6 * B, width), BF16),
            pltpu.VMEM((B, B), F32),
            pltpu.VMEM((B, B), F32),
        ],
        compiler_params=pltpu.CompilerParams(vmem_limit_bytes=VMEM_LIMIT),
        name="cholesky",
    )(shifted)


def iterate_kernel(a_ref, x_ref, o_ref, hi_ref, mid_ref, low_ref):
    width, modes = x_ref.shape
    hi_ref[...], mid_ref[...], low_ref[...] = split3(a_ref[...])
    o_ref[...] = x_ref[...]

    @pl.loop(0, ITERS)
    def sweep(_):
        x1, x2, x3 = split3(o_ref[...])
        first = lax.dot_general(
            hi_ref[...],
            jnp.concatenate([x1, x2, x3], axis=1),
            ROWCOL,
            preferred_element_type=F32,
        )
        second = lax.dot_general(
            mid_ref[...],
            jnp.concatenate([x1, x2], axis=1),
            ROWCOL,
            preferred_element_type=F32,
        )
        third = lax.dot_general(low_ref[...], x1, ROWCOL, preferred_element_type=F32)
        image = (
            (third + second[:, modes:] + first[:, 2 * modes :])
            + (first[:, modes : 2 * modes] + second[:, :modes])
            + first[:, :modes]
        )
        correlation = dot6(image, image, COL0)
        _, v = factor_block(correlation)
        o_ref[...] = dot6(image, v, COLCOL)


def iterate(shifted, start_block):
    width, modes = start_block.shape
    return pl.pallas_call(
        iterate_kernel,
        out_shape=jax.ShapeDtypeStruct((width, modes), F32),
        in_specs=[pl.BlockSpec(memory_space=pltpu.VMEM)] * 2,
        out_specs=pl.BlockSpec(memory_space=pltpu.VMEM),
        scratch_shapes=[pltpu.VMEM((width, width), BF16)] * 3,
        compiler_params=pltpu.CompilerParams(vmem_limit_bytes=VMEM_LIMIT),
        name="iterate",
    )(shifted, start_block)


def modes_kernel(m_ref, b_ref, o_ref):
    modes = b_ref.shape[1]
    b1, b2, b3 = split3(b_ref[...])
    parts = lax.dot_general(
        m_ref[...], jnp.concatenate([b1, b2, b3], axis=1), ROWCOL, preferred_element_type=F32
    )
    o_ref[...] = (parts[:, 2 * modes :] + parts[:, modes : 2 * modes]) + parts[:, :modes]


def modes_of(masked, block):
    return pl.pallas_call(
        modes_kernel,
        out_shape=jax.ShapeDtypeStruct((masked.shape[0], block.shape[1]), F32),
        in_specs=[pl.BlockSpec(memory_space=pltpu.VMEM)] * 2,
        out_specs=pl.BlockSpec(memory_space=pltpu.VMEM),
        compiler_params=pltpu.CompilerParams(vmem_limit_bytes=VMEM_LIMIT),
        name="modes",
    )(masked, block)


def active_columns(lengths, width):
    columns = jnp.arange(width, dtype=jnp.int32)
    lookup = (columns // STEPS)[:, None] == jnp.arange(PASSES, dtype=jnp.int32)[None, :]
    col_length = jnp.sum(jnp.where(lookup, lengths[None, :], 0), axis=1)
    return columns % STEPS < col_length


def body(snapshots, lengths, start_block):
    snap = lax.axis_size("snap")
    width = start_block.shape[0]
    row_count = snapshots.shape[0] * lax.axis_size("dof")
    own = lax.all_to_all(snapshots, "snap", split_axis=0, concat_axis=1, tiled=True)
    active = active_columns(lengths, width)
    masked = jnp.where(active[None, :], own, jnp.zeros_like(own))
    gram = lax.psum(
        lax.dot_general(masked, masked, COL0, preferred_element_type=F32), ("dof", "snap")
    )
    shifted = gram / F32(row_count) + 0.05 * jnp.eye(width, dtype=F32)
    first = lax.axis_index("snap") % 2 == 0
    upper, block = lax.cond(
        first,
        lambda: (cholesky(shifted), start_block),
        lambda: (shifted, iterate(shifted, start_block)),
    )
    down = [(i, i + 1) for i in range(0, snap, 2)]
    up = [(i + 1, i) for i in range(0, snap, 2)]
    upper = jnp.where(first, upper, lax.ppermute(upper, "snap", down))
    block = jnp.where(first, lax.ppermute(block, "snap", up), block)
    return modes_of(masked, block), upper


def solution(mesh):
    placed = (P("dof", "snap"), P(), P())
    return jax.shard_map(
        body, mesh=mesh, in_specs=placed, out_specs=(P(("dof", "snap"), None), P()), check_vma=False
    )
```

```python
import functools

import jax
import jax.numpy as jnp
from jax import lax
from jax.experimental import pallas as pl
from jax.experimental.pallas import tpu as pltpu
from jax.sharding import PartitionSpec as P

STEPS = 64
ITERS = 3
PASSES = 16
B = 128
VMEM_LIMIT = 48 * 1024 * 1024
F32 = jnp.float32
BF16 = jnp.bfloat16
COL0 = (((0,), (0,)), ((), ()))
ROWCOL = (((1,), (0,)), ((), ()))
COLCOL = (((1,), (1,)), ((), ()))


def split3(x):
    hi = x.astype(BF16)
    rest = x - hi.astype(F32)
    mid = rest.astype(BF16)
    low = (rest - mid.astype(F32)).astype(BF16)
    return hi, mid, low


def dot6(a, b, dims):
    return lax.dot_general(
        a, b, dims, precision=lax.Precision.HIGHEST, preferred_element_type=F32
    )


def factor_block(block):
    rows = [None] * (B // 8)
    for i in range(B // 8):
        r = lax.broadcasted_iota(jnp.int32, (8, B), 0) + 8 * i
        c = lax.broadcasted_iota(jnp.int32, (8, B), 1)
        rows[i] = (block[8 * i : 8 * i + 8, :], jnp.where(r == c, 1.0, 0.0).astype(F32))
    sub = lax.broadcasted_iota(jnp.int32, (8, B), 0)
    upper, inverse = [], []
    for g in range(B // 8):
        left, right = rows[g]
        cols = [
            jnp.broadcast_to(left[:, 8 * g + t : 8 * g + t + 1], (8, B)) for t in range(8)
        ]
        outer = [
            [
                jnp.broadcast_to(rows[i][0][:, 8 * g + t : 8 * g + t + 1], (8, B))
                for t in range(8)
            ]
            for i in range(g + 1, B // 8)
        ]
        u_tile = jnp.zeros((8, B), F32)
        v_tile = jnp.zeros((8, B), F32)
        for t in range(8):
            pivot = jnp.broadcast_to(cols[t][t : t + 1, :], (8, B))
            recip = 1.0 / pivot
            scale = lax.rsqrt(pivot)
            left_row = jnp.broadcast_to(left[t : t + 1, :], (8, B))
            right_row = jnp.broadcast_to(right[t : t + 1, :], (8, B))
            u_tile = jnp.where(sub == t, left_row * scale, u_tile)
            v_tile = jnp.where(sub == t, right_row * scale, v_tile)
            factor = jnp.where(sub == t, cols[t] - 1.0, cols[t]) * recip
            left_new = jnp.where(sub == t, left_row * recip, left - factor * left_row)
            right_new = jnp.where(sub == t, right_row * recip, right - factor * right_row)
            for c in range(t + 1, 8):
                head = jnp.broadcast_to(cols[c][t : t + 1, :], (8, B))
                cols[c] = jnp.where(sub == t, head * recip, cols[c] - factor * head)
            left, right = left_new, right_new
        upper.append(u_tile)
        inverse.append(v_tile)
        left_rows = [jnp.broadcast_to(left[t : t + 1, :], (8, B)) for t in range(8)]
        right_rows = [jnp.broadcast_to(right[t : t + 1, :], (8, B)) for t in range(8)]
        for i in range(g + 1, B // 8):
            a, b = rows[i]
            coef = outer[i - g - 1]
            for t in range(8):
                a = a - coef[t] * left_rows[t]
                b = b - coef[t] * right_rows[t]
            rows[i] = (a, b)
    u = jnp.concatenate(upper, axis=0)
    v = jnp.concatenate(inverse, axis=0)
    r = lax.broadcasted_iota(jnp.int32, (B, B), 0)
    c = lax.broadcasted_iota(jnp.int32, (B, B), 1)
    return jnp.where(c >= r, u, 0.0), v


MESH = pl.DeviceIdType.MESH


def block_rows(i, j, count):
    return (i * count - i * (i - 1) // 2 + (j - i)) * B


def packed_rows(count, devices):
    chunk = -(-(count * (count + 1) // 2 * B) // (8 * devices)) * 8
    return chunk * devices


def stages_of(dofs, snaps):
    d, s = lax.axis_index("dof"), lax.axis_index("snap")
    core, x, y = s % 2, d % 2, (s // 2) % 2
    stages = [(core, 2, lambda j: (d, s + 1 - 2 * core))]
    rest = 1 - core
    if snaps == 4 and dofs % 2 == 0:
        stages.append(
            (
                rest * x + core * y,
                2,
                lambda j: (d + rest * (1 - 2 * x), s + core * 2 * (1 - 2 * y)),
            )
        )
        stages.append(
            (
                rest * y + core * x,
                2,
                lambda j: (d + core * (1 - 2 * x), s + rest * 2 * (1 - 2 * y)),
            )
        )
        stride = 2
    else:
        wide = snaps // 2
        if wide > 1:
            high = s // 2
            stages.append((high, wide, lambda j: (d, s + 2 * ((high + j) % wide - high))))
        stride = 1
    while stride < dofs:
        left = dofs // stride
        radix = 4 if left % 4 == 0 else 2 if left % 2 == 0 else left
        digit = (d // stride) % radix
        stages.append(
            (
                digit,
                radix,
                lambda j, g=digit, r=radix, t=stride: (d + t * ((g + j) % r - g), s),
            )
        )
        stride *= radix
    return stages


def gram_kernel(
    dofs, snaps, x_ref, active_ref, m_ref, g_ref, slots, part, total, *rest
):
    landing, sems = rest[:-4], rest[-4:]
    swap_sems, own_sem, send_sems, recv_sems = sems
    d, s = lax.axis_index("dof"), lax.axis_index("snap")
    stages = stages_of(dofs, snaps)
    rows, panel = slots.shape[1], slots.shape[2]
    width = m_ref.shape[1]
    count = width // B

    peers = [(d, (s + j) % snaps) for j in range(1, snaps)]
    barrier = pltpu.get_barrier_semaphore()
    if snaps == 4 and dofs % 2 == 0:
        greet = list(peers) + [(d + 1 - 2 * (d % 2), s)]
        for _, radix, peer in stages[3:]:
            greet += [peer(j) for j in range(1, radix)]
    else:
        greet = list(peers)
        for _, radix, peer in stages[1 + (snaps > 2) :]:
            greet += [peer(j) for j in range(1, radix)]
    for device in greet:
        pl.semaphore_signal(barrier, inc=1, device_id=device, device_id_type=MESH)
    pl.semaphore_wait(barrier, len(greet))

    swaps = []
    for j in range(1, snaps):
        target = (s + j) % snaps
        copy = pltpu.make_async_remote_copy(
            src_ref=x_ref.at[pl.ds(pl.multiple_of(target * rows, 16), rows), :],
            dst_ref=slots.at[s],
            send_sem=swap_sems.at[0, j],
            recv_sem=swap_sems.at[1, j],
            device_id=(d, target),
            device_id_type=MESH,
        )
        copy.start()
        swaps.append(copy)
    own = pltpu.make_async_copy(
        x_ref.at[pl.ds(pl.multiple_of(s * rows, 16), rows), :], slots.at[s], own_sem
    )
    own.start()
    own.wait()
    for copy in swaps:
        copy.wait_recv()
    for i in range(snaps):
        columns = slice(i * panel, (i + 1) * panel)
        m_ref[:, columns] = (
            slots[i].astype(F32) * active_ref[0:1, columns]
        ).astype(BF16)

    for i in range(count):
        strip = lax.dot_general(
            m_ref[:, i * B : (i + 1) * B],
            m_ref[:, i * B :],
            COL0,
            preferred_element_type=F32,
        )
        for j in range(i, count):
            first = block_rows(i, j, count)
            part[first : first + B, :] = strip[:, (j - i) * B : (j - i + 1) * B]
    end = block_rows(count - 1, count - 1, count) + B
    if end < part.shape[0]:
        part[end:, :] = jnp.zeros((part.shape[0] - end, B), F32)
    for copy in swaps:
        copy.wait_send()

    offset, length = 0, part.shape[0]
    spans = []
    for n, (digit, radix, peer) in enumerate(stages):
        size = length // radix
        copies = []
        for j in range(1, radix):
            there = offset + ((digit + j) % radix) * size
            copy = pltpu.make_async_remote_copy(
                src_ref=part.at[pl.ds(pl.multiple_of(there, 8), size), :],
                dst_ref=landing[n].at[j - 1],
                send_sem=send_sems.at[0, n, j],
                recv_sem=recv_sems.at[0, n, j],
                device_id=peer(j),
                device_id_type=MESH,
            )
            copy.start()
            copies.append(copy)
        offset = offset + digit * size
        length = size
        spans.append((offset, size))
        here = pl.ds(pl.multiple_of(offset, 8), size)
        for copy in copies:
            copy.wait_recv()
        value = part[here, :]
        for j in range(1, radix):
            value = value + landing[n][j - 1]
        if n == len(stages) - 1:
            total[here, :] = value
        else:
            part[here, :] = value
        for copy in copies:
            copy.wait_send()

    for n in reversed(range(len(stages))):
        _, radix, peer = stages[n]
        start, size = spans[n]
        here = pl.ds(pl.multiple_of(start, 8), size)
        copies = []
        for j in range(1, radix):
            copy = pltpu.make_async_remote_copy(
                src_ref=total.at[here, :],
                dst_ref=total.at[here, :],
                send_sem=send_sems.at[1, n, j],
                recv_sem=recv_sems.at[1, n, j],
                device_id=peer(j),
                device_id_type=MESH,
            )
            copy.start()
            copies.append(copy)
        for copy in copies:
            copy.wait_recv()
        for copy in copies:
            copy.wait_send()
    g_ref[...] = total[...]


def gram_of(snapshots, active, dofs, snaps):
    rows, panel = snapshots.shape[0] // snaps, snapshots.shape[1]
    width = panel * snaps
    packed = packed_rows(width // B, dofs * snaps)
    radices = [2]
    if snaps == 4 and dofs % 2 == 0:
        radices += [2, 2]
        stride = 2
    else:
        radices += [snaps // 2] if snaps > 2 else []
        stride = 1
    while stride < dofs:
        left = dofs // stride
        radices.append(4 if left % 4 == 0 else 2 if left % 2 == 0 else left)
        stride *= radices[-1]
    landing, length = [], packed
    for radix in radices:
        length //= radix
        landing.append(pltpu.VMEM((radix - 1, length, B), F32))
    most = max(radices)
    return pl.pallas_call(
        functools.partial(gram_kernel, dofs, snaps),
        out_shape=(
            jax.ShapeDtypeStruct((rows, width), BF16),
            jax.ShapeDtypeStruct((packed, B), F32),
        ),
        in_specs=[
            pl.BlockSpec(memory_space=pl.ANY),
            pl.BlockSpec(memory_space=pltpu.VMEM),
        ],
        out_specs=(pl.BlockSpec(memory_space=pltpu.VMEM),) * 2,
        scratch_shapes=[
            pltpu.VMEM((snaps, rows, panel), BF16),
            pltpu.VMEM((packed, B), F32),
            pltpu.VMEM((packed, B), F32),
            *landing,
            pltpu.SemaphoreType.DMA((2, snaps)),
            pltpu.SemaphoreType.DMA,
            pltpu.SemaphoreType.DMA((2, len(radices), most)),
            pltpu.SemaphoreType.DMA((2, len(radices), most)),
        ],
        compiler_params=pltpu.CompilerParams(
            collective_id=0, has_side_effects=True, vmem_limit_bytes=VMEM_LIMIT
        ),
        name="gram",
    )(snapshots, active)


def shifted_block(g_ref, i, j, count, row_count):
    first = block_rows(i, j, count)
    block = g_ref[first : first + B, :] / F32(row_count)
    if i == j:
        r = lax.broadcasted_iota(jnp.int32, (B, B), 0)
        c = lax.broadcasted_iota(jnp.int32, (B, B), 1)
        block = block + jnp.where(r == c, 0.05, 0.0).astype(F32)
    return block


def cholesky_kernel(row_count, g_ref, r_ref, left_ref, right_ref):
    width = r_ref.shape[0]
    count = width // B
    for i in range(count):
        r_ref[i * B : (i + 1) * B, :] = jnp.zeros((B, width), F32)
        for j in range(i, count):
            r_ref[i * B : (i + 1) * B, j * B : (j + 1) * B] = shifted_block(
                g_ref, i, j, count, row_count
            )

    @pl.loop(0, count)
    def panel(k):
        here = pl.ds(pl.multiple_of(k * B, B), B)
        u, v = factor_block(r_ref[here, here])
        row = dot6(v, r_ref[here, :], ROWCOL)
        col = lax.broadcasted_iota(jnp.int32, (B, width), 1)
        row = jnp.where(col >= (k + 1) * B, row, 0.0)
        r_ref[here, :] = row
        r_ref[here, here] = u
        hi, mid, low = split3(row)
        left_ref[...] = jnp.concatenate([hi, mid, hi, low, mid, hi], axis=0)
        right_ref[...] = jnp.concatenate([hi, hi, mid, hi, mid, low], axis=0)

        @pl.loop(k + 1, count)
        def update(i):
            there = pl.ds(pl.multiple_of(i * B, B), B)
            r_ref[there, :] = r_ref[there, :] - lax.dot_general(
                left_ref[:, there], right_ref[...], COL0, preferred_element_type=F32
            )


def cholesky(packed, width, row_count):
    return pl.pallas_call(
        functools.partial(cholesky_kernel, row_count),
        out_shape=jax.ShapeDtypeStruct((width, width), F32),
        in_specs=[pl.BlockSpec(memory_space=pltpu.VMEM)],
        out_specs=pl.BlockSpec(memory_space=pltpu.VMEM),
        scratch_shapes=[
            pltpu.VMEM((6 * B, width), BF16),
            pltpu.VMEM((6 * B, width), BF16),
        ],
        compiler_params=pltpu.CompilerParams(vmem_limit_bytes=VMEM_LIMIT),
        name="cholesky",
    )(packed)


def iterate_kernel(row_count, g_ref, x_ref, o_ref, hi_ref, mid_ref, low_ref):
    width, modes = x_ref.shape
    count = width // B
    for i in range(count):
        for j in range(i, count):
            block = shifted_block(g_ref, i, j, count, row_count)
            a, b = slice(i * B, (i + 1) * B), slice(j * B, (j + 1) * B)
            hi_ref[a, b], mid_ref[a, b], low_ref[a, b] = split3(block)
            if i < j:
                hi_ref[b, a], mid_ref[b, a], low_ref[b, a] = split3(block.T)
    o_ref[...] = x_ref[...]

    @pl.loop(0, ITERS)
    def sweep(_):
        x1, x2, x3 = split3(o_ref[...])
        first = lax.dot_general(
            hi_ref[...],
            jnp.concatenate([x1, x2, x3], axis=1),
            ROWCOL,
            preferred_element_type=F32,
        )
        second = lax.dot_general(
            mid_ref[...],
            jnp.concatenate([x1, x2], axis=1),
            ROWCOL,
            preferred_element_type=F32,
        )
        third = lax.dot_general(low_ref[...], x1, ROWCOL, preferred_element_type=F32)
        image = (
            (third + second[:, modes:] + first[:, 2 * modes :])
            + (first[:, modes : 2 * modes] + second[:, :modes])
            + first[:, :modes]
        )
        correlation = dot6(image, image, COL0)
        _, v = factor_block(correlation)
        o_ref[...] = dot6(image, v, COLCOL)


def iterate(packed, start_block, row_count):
    width, modes = start_block.shape
    return pl.pallas_call(
        functools.partial(iterate_kernel, row_count),
        out_shape=jax.ShapeDtypeStruct((width, modes), F32),
        in_specs=[pl.BlockSpec(memory_space=pltpu.VMEM)] * 2,
        out_specs=pl.BlockSpec(memory_space=pltpu.VMEM),
        scratch_shapes=[pltpu.VMEM((width, width), BF16)] * 3,
        compiler_params=pltpu.CompilerParams(vmem_limit_bytes=VMEM_LIMIT),
        name="iterate",
    )(packed, start_block)


def modes_kernel(m_ref, b_ref, o_ref):
    modes = b_ref.shape[1]
    b1, b2, b3 = split3(b_ref[...])
    parts = lax.dot_general(
        m_ref[...], jnp.concatenate([b1, b2, b3], axis=1), ROWCOL, preferred_element_type=F32
    )
    o_ref[...] = (parts[:, 2 * modes :] + parts[:, modes : 2 * modes]) + parts[:, :modes]


def modes_of(masked, block):
    return pl.pallas_call(
        modes_kernel,
        out_shape=jax.ShapeDtypeStruct((masked.shape[0], block.shape[1]), F32),
        in_specs=[pl.BlockSpec(memory_space=pltpu.VMEM)] * 2,
        out_specs=pl.BlockSpec(memory_space=pltpu.VMEM),
        compiler_params=pltpu.CompilerParams(vmem_limit_bytes=VMEM_LIMIT),
        name="modes",
    )(masked, block)


def active_columns(lengths, width):
    columns = jnp.arange(width, dtype=jnp.int32)
    lookup = (columns // STEPS)[:, None] == jnp.arange(PASSES, dtype=jnp.int32)[None, :]
    col_length = jnp.sum(jnp.where(lookup, lengths[None, :], 0), axis=1)
    return columns % STEPS < col_length


def body(snapshots, lengths, start_block):
    dofs, snap = lax.axis_size("dof"), lax.axis_size("snap")
    width = start_block.shape[0]
    row_count = snapshots.shape[0] * dofs
    active = jnp.broadcast_to(active_columns(lengths, width).astype(F32)[None, :], (8, width))
    masked, packed = gram_of(snapshots, active, dofs, snap)
    first = lax.axis_index("snap") % 2 == 0
    upper, block = lax.cond(
        first,
        lambda: (cholesky(packed, width, row_count), start_block),
        lambda: (jnp.zeros((width, width), F32), iterate(packed, start_block, row_count)),
    )
    down = [(i, i + 1) for i in range(0, snap, 2)]
    up = [(i + 1, i) for i in range(0, snap, 2)]
    upper = jnp.where(first, upper, lax.ppermute(upper, "snap", down))
    block = jnp.where(first, lax.ppermute(block, "snap", up), block)
    return modes_of(masked, block), upper


def solution(mesh):
    placed = (P("dof", "snap"), P(), P())
    return jax.shard_map(
        body, mesh=mesh, in_specs=placed, out_specs=(P(("dof", "snap"), None), P()), check_vma=False
    )
```

```python
import functools

import jax
import jax.numpy as jnp
from jax import lax
from jax.experimental import pallas as pl
from jax.experimental.pallas import tpu as pltpu
from jax.sharding import PartitionSpec as P

STEPS = 64
ITERS = 3
PASSES = 16
B = 128
VMEM_LIMIT = 48 * 1024 * 1024
F32 = jnp.float32
BF16 = jnp.bfloat16
COL0 = (((0,), (0,)), ((), ()))
ROWCOL = (((1,), (0,)), ((), ()))
COLCOL = (((1,), (1,)), ((), ()))


def split3(x):
    hi = x.astype(BF16)
    rest = x - hi.astype(F32)
    mid = rest.astype(BF16)
    low = (rest - mid.astype(F32)).astype(BF16)
    return hi, mid, low


def dot6(a, b, dims):
    return lax.dot_general(
        a, b, dims, precision=lax.Precision.HIGHEST, preferred_element_type=F32
    )


def factor_block(block):
    rows = [None] * (B // 8)
    for i in range(B // 8):
        r = lax.broadcasted_iota(jnp.int32, (8, B), 0) + 8 * i
        c = lax.broadcasted_iota(jnp.int32, (8, B), 1)
        rows[i] = (block[8 * i : 8 * i + 8, :], jnp.where(r == c, 1.0, 0.0).astype(F32))
    sub = lax.broadcasted_iota(jnp.int32, (8, B), 0)
    upper, inverse = [], []
    for g in range(B // 8):
        left, right = rows[g]
        cols = [
            jnp.broadcast_to(left[:, 8 * g + t : 8 * g + t + 1], (8, B)) for t in range(8)
        ]
        outer = [
            [
                jnp.broadcast_to(rows[i][0][:, 8 * g + t : 8 * g + t + 1], (8, B))
                for t in range(8)
            ]
            for i in range(g + 1, B // 8)
        ]
        u_tile = jnp.zeros((8, B), F32)
        v_tile = jnp.zeros((8, B), F32)
        for t in range(8):
            pivot = jnp.broadcast_to(cols[t][t : t + 1, :], (8, B))
            recip = 1.0 / pivot
            scale = lax.rsqrt(pivot)
            left_row = jnp.broadcast_to(left[t : t + 1, :], (8, B))
            right_row = jnp.broadcast_to(right[t : t + 1, :], (8, B))
            u_tile = jnp.where(sub == t, left_row * scale, u_tile)
            v_tile = jnp.where(sub == t, right_row * scale, v_tile)
            factor = jnp.where(sub == t, cols[t] - 1.0, cols[t]) * recip
            left_new = jnp.where(sub == t, left_row * recip, left - factor * left_row)
            right_new = jnp.where(sub == t, right_row * recip, right - factor * right_row)
            for c in range(t + 1, 8):
                head = jnp.broadcast_to(cols[c][t : t + 1, :], (8, B))
                cols[c] = jnp.where(sub == t, head * recip, cols[c] - factor * head)
            left, right = left_new, right_new
        upper.append(u_tile)
        inverse.append(v_tile)
        left_rows = [jnp.broadcast_to(left[t : t + 1, :], (8, B)) for t in range(8)]
        right_rows = [jnp.broadcast_to(right[t : t + 1, :], (8, B)) for t in range(8)]
        for i in range(g + 1, B // 8):
            a, b = rows[i]
            coef = outer[i - g - 1]
            for t in range(8):
                a = a - coef[t] * left_rows[t]
                b = b - coef[t] * right_rows[t]
            rows[i] = (a, b)
    u = jnp.concatenate(upper, axis=0)
    v = jnp.concatenate(inverse, axis=0)
    r = lax.broadcasted_iota(jnp.int32, (B, B), 0)
    c = lax.broadcasted_iota(jnp.int32, (B, B), 1)
    return jnp.where(c >= r, u, 0.0), v


MESH = pl.DeviceIdType.MESH


def padded(blocks, devices):
    return -(-blocks * B // (8 * devices)) * 8 * devices


def layout(count, dofs):
    half = count // 2
    return padded(half * (half + 1) // 2, 2 * dofs), padded(half * half, 4 * dofs)


def triangle(i, j, half):
    return (i * half - i * (i - 1) // 2 + (j - i)) * B


def block_rows(i, j, count, dofs):
    half = count // 2
    near, _ = layout(count, dofs)
    if j < half:
        return triangle(i, j, half)
    if i >= half:
        return near + triangle(i - half, j - half, half)
    return 2 * near + (i * half + j - half) * B


def radices_of(dofs):
    found = []
    left = dofs
    while left > 1:
        found.append(2 if not found else 4 if left % 4 == 0 else 2 if left % 2 == 0 else left)
        left //= found[-1]
    return found


def far_stages(dofs, first):
    d, s = lax.axis_index("dof"), lax.axis_index("snap")
    stages, stride = [], 1
    for n, radix in enumerate(radices_of(dofs)):
        digit = (d // stride) % radix
        if n >= first:
            stages.append(
                (
                    digit,
                    radix,
                    lambda j, g=digit, r=radix, t=stride: (d + t * ((g + j) % r - g), s),
                )
            )
        stride *= radix
    return stages


def gram_kernel(dofs, x_ref, active_ref, m_ref, g_ref, *scratch):
    slots, extra, near_ref, part1, part2, diag, total, own_sems, send_sems, recv_sems = scratch[:10]
    landing = list(scratch[10:])
    d, s = lax.axis_index("dof"), lax.axis_index("snap")
    core, y, x = s % 2, s // 2, d % 2
    rest = 1 - core
    rows, panel = slots.shape[1], slots.shape[2]
    width = m_ref.shape[1]
    count = width // B
    half = count // 2
    near = part1.shape[0]
    cross = part2.shape[0]
    beside, over, across = s + 1 - 2 * core, (s + 2) % 4, (s + 1 - 2 * core + 2) % 4
    pair = (core, 2, lambda j: (d, beside))
    dof_stages = far_stages(dofs, 0)
    stages1 = [pair] + dof_stages
    stages2 = [
        pair,
        (
            rest * x + core * y,
            2,
            lambda j: (d + rest * (1 - 2 * x), s + core * 2 * (1 - 2 * y)),
        ),
        (
            rest * y + core * x,
            2,
            lambda j: (d + core * (1 - 2 * x), s + rest * 2 * (1 - 2 * y)),
        ),
    ] + dof_stages[1:]

    greet = [(d, beside), (d, over), (d, across)]
    for _, radix, peer in dof_stages:
        greet += [peer(j) for j in range(1, radix)]
    barrier = pltpu.get_barrier_semaphore()
    for device in greet:
        pl.semaphore_signal(barrier, inc=1, device_id=device, device_id_type=MESH)
    pl.semaphore_wait(barrier, len(greet))

    used = []

    def send(src, dst, device):
        n = len(used)
        used.append(n)
        copy = pltpu.make_async_remote_copy(
            src_ref=src,
            dst_ref=dst,
            send_sem=send_sems.at[n],
            recv_sem=recv_sems.at[n],
            device_id=device,
            device_id_type=MESH,
        )
        copy.start()
        return copy

    def quarter(q):
        return x_ref.at[pl.ds(pl.multiple_of(q * rows, 16), rows), :]

    def span(offset, size):
        return pl.ds(pl.multiple_of(offset, 8), size)

    def scatter(stages, part, put):
        offset, length = 0, part.shape[0]
        spans = []
        for n, (digit, radix, peer) in enumerate(stages):
            size = length // radix
            arrive = landing.pop(0)
            copies = [
                send(
                    part.at[span(offset + ((digit + j) % radix) * size, size), :],
                    arrive.at[j - 1],
                    peer(j),
                )
                for j in range(1, radix)
            ]
            offset, length = offset + digit * size, size
            spans.append((offset, size))
            for copy in copies:
                copy.wait_recv()
            value = part[span(offset, size), :]
            for j in range(1, radix):
                value = value + arrive[j - 1]
            if n == len(stages) - 1:
                put(span(offset, size), value)
            else:
                part[span(offset, size), :] = value
            for copy in copies:
                copy.wait_send()
        return spans

    def gather(stages, spans, view):
        for n in reversed(range(len(stages))):
            _, radix, peer = stages[n]
            here = view(span(*spans[n]))
            copies = [send(here, here, peer(j)) for j in range(1, radix)]
            for copy in copies:
                copy.wait_recv()
            for copy in copies:
                copy.wait_send()

    pair_copies = [
        send(quarter(beside), slots.at[s], (d, beside)),
        send(quarter(across), extra.at[core], (d, beside)),
    ]
    far_copies = [
        send(quarter(over), slots.at[s], (d, over)),
        send(quarter(across), slots.at[s], (d, across)),
    ]
    own = [
        pltpu.make_async_copy(quarter(s), slots.at[s], own_sems.at[0]),
        pltpu.make_async_copy(quarter(over), extra.at[core], own_sems.at[1]),
    ]
    for copy in own:
        copy.start()
    for copy in own:
        copy.wait()
    for copy in pair_copies:
        copy.wait_recv()

    for i in range(2):
        columns = slice(i * panel, (i + 1) * panel)
        q = 2 * y + i
        keep = active_ref[0:1, pl.ds(pl.multiple_of(q * panel, panel), panel)]
        near_ref[:rows, columns] = (slots[q].astype(F32) * keep).astype(BF16)
        near_ref[rows:, columns] = (extra[i].astype(F32) * keep).astype(BF16)
    for i in range(half):
        strip = lax.dot_general(
            near_ref[:, i * B : (i + 1) * B],
            near_ref[:, i * B :],
            COL0,
            preferred_element_type=F32,
        )
        for j in range(i, half):
            first = triangle(i, j, half)
            part1[first : first + B, :] = strip[:, (j - i) * B : (j - i + 1) * B]
    end = half * (half + 1) // 2 * B
    if end < near:
        part1[end:, :] = jnp.zeros((near - end, B), F32)

    def put_diag(here, value):
        diag[y, here, :] = value

    spans = scatter(stages1, part1, put_diag)
    gather(stages1, spans, lambda here: diag.at[y, here, :])
    mine = span(core * (near // 2), near // 2)
    swap = send(diag.at[y, mine, :], diag.at[y, mine, :], (d, over))

    for copy in far_copies:
        copy.wait_recv()
    for i in range(4):
        columns = slice(i * panel, (i + 1) * panel)
        m_ref[:, columns] = (
            slots[i].astype(F32) * active_ref[0:1, columns]
        ).astype(BF16)
    for i in range(half):
        strip = lax.dot_general(
            m_ref[:, i * B : (i + 1) * B],
            m_ref[:, half * B :],
            COL0,
            preferred_element_type=F32,
        )
        for j in range(half):
            first = (i * half + j) * B
            part2[first : first + B, :] = strip[:, j * B : (j + 1) * B]
    end = half * half * B
    if end < cross:
        part2[end:, :] = jnp.zeros((cross - end, B), F32)

    def put_total(here, value):
        total[here, :] = value

    spans = scatter(stages2, part2, put_total)
    swap.wait_recv()
    other = diag.at[1 - y, mine, :]
    share = send(other, other, (d, beside))
    gather(stages2, spans, lambda here: total.at[here, :])
    share.wait_recv()
    g_ref[:near, :] = diag[0]
    g_ref[near : 2 * near, :] = diag[1]
    g_ref[2 * near :, :] = total[...]
    for copy in [*pair_copies, *far_copies, swap, share]:
        copy.wait_send()


def gram_of(snapshots, active, dofs, snaps):
    rows, panel = snapshots.shape[0] // snaps, snapshots.shape[1]
    width = panel * snaps
    near, cross = layout(width // B, dofs)
    far = radices_of(dofs)
    landing, copies = [], 6
    for radices, length in (([2] + far, near), ([2, 2] + far, cross)):
        for radix in radices:
            length //= radix
            landing.append(pltpu.VMEM((radix - 1, length, B), F32))
            copies += 2 * (radix - 1)
    return pl.pallas_call(
        functools.partial(gram_kernel, dofs),
        out_shape=(
            jax.ShapeDtypeStruct((rows, width), BF16),
            jax.ShapeDtypeStruct((2 * near + cross, B), F32),
        ),
        in_specs=[
            pl.BlockSpec(memory_space=pl.ANY),
            pl.BlockSpec(memory_space=pltpu.VMEM),
        ],
        out_specs=(pl.BlockSpec(memory_space=pltpu.VMEM),) * 2,
        scratch_shapes=[
            pltpu.VMEM((snaps, rows, panel), BF16),
            pltpu.VMEM((2, rows, panel), BF16),
            pltpu.VMEM((2 * rows, 2 * panel), BF16),
            pltpu.VMEM((near, B), F32),
            pltpu.VMEM((cross, B), F32),
            pltpu.VMEM((2, near, B), F32),
            pltpu.VMEM((cross, B), F32),
            pltpu.SemaphoreType.DMA((2,)),
            pltpu.SemaphoreType.DMA((copies,)),
            pltpu.SemaphoreType.DMA((copies,)),
            *landing,
        ],
        compiler_params=pltpu.CompilerParams(
            collective_id=0, has_side_effects=True, vmem_limit_bytes=VMEM_LIMIT
        ),
        name="gram",
    )(snapshots, active)


def shifted_block(g_ref, i, j, count, dofs, row_count):
    first = block_rows(i, j, count, dofs)
    block = g_ref[first : first + B, :] / F32(row_count)
    if i == j:
        r = lax.broadcasted_iota(jnp.int32, (B, B), 0)
        c = lax.broadcasted_iota(jnp.int32, (B, B), 1)
        block = block + jnp.where(r == c, 0.05, 0.0).astype(F32)
    return block


def cholesky_kernel(dofs, row_count, g_ref, r_ref, left_ref, right_ref):
    width = r_ref.shape[0]
    count = width // B
    for i in range(count):
        r_ref[i * B : (i + 1) * B, :] = jnp.zeros((B, width), F32)
        for j in range(i, count):
            r_ref[i * B : (i + 1) * B, j * B : (j + 1) * B] = shifted_block(
                g_ref, i, j, count, dofs, row_count
            )

    @pl.loop(0, count)
    def panel(k):
        here = pl.ds(pl.multiple_of(k * B, B), B)
        u, v = factor_block(r_ref[here, here])
        row = dot6(v, r_ref[here, :], ROWCOL)
        col = lax.broadcasted_iota(jnp.int32, (B, width), 1)
        row = jnp.where(col >= (k + 1) * B, row, 0.0)
        r_ref[here, :] = row
        r_ref[here, here] = u
        hi, mid, low = split3(row)
        left_ref[...] = jnp.concatenate([hi, mid, hi, low, mid, hi], axis=0)
        right_ref[...] = jnp.concatenate([hi, hi, mid, hi, mid, low], axis=0)

        @pl.loop(k + 1, count)
        def update(i):
            there = pl.ds(pl.multiple_of(i * B, B), B)
            r_ref[there, :] = r_ref[there, :] - lax.dot_general(
                left_ref[:, there], right_ref[...], COL0, preferred_element_type=F32
            )


def cholesky(packed, width, dofs, row_count):
    return pl.pallas_call(
        functools.partial(cholesky_kernel, dofs, row_count),
        out_shape=jax.ShapeDtypeStruct((width, width), F32),
        in_specs=[pl.BlockSpec(memory_space=pltpu.VMEM)],
        out_specs=pl.BlockSpec(memory_space=pltpu.VMEM),
        scratch_shapes=[
            pltpu.VMEM((6 * B, width), BF16),
            pltpu.VMEM((6 * B, width), BF16),
        ],
        compiler_params=pltpu.CompilerParams(vmem_limit_bytes=VMEM_LIMIT),
        name="cholesky",
    )(packed)


def iterate_kernel(dofs, row_count, g_ref, x_ref, o_ref, hi_ref, mid_ref, low_ref):
    width, modes = x_ref.shape
    count = width // B
    for i in range(count):
        for j in range(i, count):
            block = shifted_block(g_ref, i, j, count, dofs, row_count)
            a, b = slice(i * B, (i + 1) * B), slice(j * B, (j + 1) * B)
            hi_ref[a, b], mid_ref[a, b], low_ref[a, b] = split3(block)
            if i < j:
                hi_ref[b, a], mid_ref[b, a], low_ref[b, a] = split3(block.T)
    o_ref[...] = x_ref[...]

    @pl.loop(0, ITERS)
    def sweep(_):
        x1, x2, x3 = split3(o_ref[...])
        first = lax.dot_general(
            hi_ref[...],
            jnp.concatenate([x1, x2, x3], axis=1),
            ROWCOL,
            preferred_element_type=F32,
        )
        second = lax.dot_general(
            mid_ref[...],
            jnp.concatenate([x1, x2], axis=1),
            ROWCOL,
            preferred_element_type=F32,
        )
        third = lax.dot_general(low_ref[...], x1, ROWCOL, preferred_element_type=F32)
        image = (
            (third + second[:, modes:] + first[:, 2 * modes :])
            + (first[:, modes : 2 * modes] + second[:, :modes])
            + first[:, :modes]
        )
        correlation = dot6(image, image, COL0)
        _, v = factor_block(correlation)
        o_ref[...] = dot6(image, v, COLCOL)


def iterate(packed, start_block, dofs, row_count):
    width, modes = start_block.shape
    return pl.pallas_call(
        functools.partial(iterate_kernel, dofs, row_count),
        out_shape=jax.ShapeDtypeStruct((width, modes), F32),
        in_specs=[pl.BlockSpec(memory_space=pltpu.VMEM)] * 2,
        out_specs=pl.BlockSpec(memory_space=pltpu.VMEM),
        scratch_shapes=[pltpu.VMEM((width, width), BF16)] * 3,
        compiler_params=pltpu.CompilerParams(vmem_limit_bytes=VMEM_LIMIT),
        name="iterate",
    )(packed, start_block)


def modes_kernel(m_ref, b_ref, o_ref):
    modes = b_ref.shape[1]
    b1, b2, b3 = split3(b_ref[...])
    parts = lax.dot_general(
        m_ref[...], jnp.concatenate([b1, b2, b3], axis=1), ROWCOL, preferred_element_type=F32
    )
    o_ref[...] = (parts[:, 2 * modes :] + parts[:, modes : 2 * modes]) + parts[:, :modes]


def modes_of(masked, block):
    return pl.pallas_call(
        modes_kernel,
        out_shape=jax.ShapeDtypeStruct((masked.shape[0], block.shape[1]), F32),
        in_specs=[pl.BlockSpec(memory_space=pltpu.VMEM)] * 2,
        out_specs=pl.BlockSpec(memory_space=pltpu.VMEM),
        compiler_params=pltpu.CompilerParams(vmem_limit_bytes=VMEM_LIMIT),
        name="modes",
    )(masked, block)


def active_columns(lengths, width):
    columns = jnp.arange(width, dtype=jnp.int32)
    lookup = (columns // STEPS)[:, None] == jnp.arange(PASSES, dtype=jnp.int32)[None, :]
    col_length = jnp.sum(jnp.where(lookup, lengths[None, :], 0), axis=1)
    return columns % STEPS < col_length


def body(snapshots, lengths, start_block):
    dofs, snap = lax.axis_size("dof"), lax.axis_size("snap")
    width = start_block.shape[0]
    row_count = snapshots.shape[0] * dofs
    active = jnp.broadcast_to(active_columns(lengths, width).astype(F32)[None, :], (8, width))
    masked, packed = gram_of(snapshots, active, dofs, snap)
    first = lax.axis_index("snap") % 2 == 0
    upper, block = lax.cond(
        first,
        lambda: (cholesky(packed, width, dofs, row_count), start_block),
        lambda: (jnp.zeros((width, width), F32), iterate(packed, start_block, dofs, row_count)),
    )
    down = [(i, i + 1) for i in range(0, snap, 2)]
    up = [(i + 1, i) for i in range(0, snap, 2)]
    upper = jnp.where(first, upper, lax.ppermute(upper, "snap", down))
    block = jnp.where(first, lax.ppermute(block, "snap", up), block)
    return modes_of(masked, block), upper


def solution(mesh):
    placed = (P("dof", "snap"), P(), P())
    return jax.shard_map(
        body, mesh=mesh, in_specs=placed, out_specs=(P(("dof", "snap"), None), P()), check_vma=False
    )
```

```python
import functools

import jax
import jax.numpy as jnp
from jax import lax
from jax.experimental import pallas as pl
from jax.experimental.pallas import tpu as pltpu
from jax.sharding import PartitionSpec as P

STEPS = 64
ITERS = 3
PASSES = 16
B = 128
G = 16
VMEM_LIMIT = 48 * 1024 * 1024
F32 = jnp.float32
BF16 = jnp.bfloat16
COL0 = (((0,), (0,)), ((), ()))
ROWCOL = (((1,), (0,)), ((), ()))
COLCOL = (((1,), (1,)), ((), ()))


def split3(x):
    hi = x.astype(BF16)
    rest = x - hi.astype(F32)
    mid = rest.astype(BF16)
    low = (rest - mid.astype(F32)).astype(BF16)
    return hi, mid, low


def dot6(a, b, dims):
    return lax.dot_general(
        a, b, dims, precision=lax.Precision.HIGHEST, preferred_element_type=F32
    )


def factor_block(block):
    rows = [None] * (B // G)
    for i in range(B // G):
        r = lax.broadcasted_iota(jnp.int32, (G, B), 0) + G * i
        c = lax.broadcasted_iota(jnp.int32, (G, B), 1)
        rows[i] = (block[G * i : G * i + G, :], jnp.where(r == c, 1.0, 0.0).astype(F32))
    sub = lax.broadcasted_iota(jnp.int32, (G, B), 0)
    upper, inverse = [], []
    for g in range(B // G):
        left, right = rows[g]
        cols = [
            jnp.broadcast_to(left[:, G * g + t : G * g + t + 1], (G, B)) for t in range(G)
        ]
        outer = [
            [
                jnp.broadcast_to(rows[i][0][:, G * g + t : G * g + t + 1], (G, B))
                for t in range(G)
            ]
            for i in range(g + 1, B // G)
        ]
        u_tile = jnp.zeros((G, B), F32)
        v_tile = jnp.zeros((G, B), F32)
        for t in range(G):
            pivot = jnp.broadcast_to(cols[t][t : t + 1, :], (G, B))
            recip = 1.0 / pivot
            scale = lax.rsqrt(pivot)
            left_row = jnp.broadcast_to(left[t : t + 1, :], (G, B))
            right_row = jnp.broadcast_to(right[t : t + 1, :], (G, B))
            u_tile = jnp.where(sub == t, left_row * scale, u_tile)
            v_tile = jnp.where(sub == t, right_row * scale, v_tile)
            factor = jnp.where(sub == t, cols[t] - 1.0, cols[t]) * recip
            left_new = jnp.where(sub == t, left_row * recip, left - factor * left_row)
            right_new = jnp.where(sub == t, right_row * recip, right - factor * right_row)
            for c in range(t + 1, G):
                head = jnp.broadcast_to(cols[c][t : t + 1, :], (G, B))
                cols[c] = jnp.where(sub == t, head * recip, cols[c] - factor * head)
            left, right = left_new, right_new
        upper.append(u_tile)
        inverse.append(v_tile)
        left_rows = [jnp.broadcast_to(left[t : t + 1, :], (G, B)) for t in range(G)]
        right_rows = [jnp.broadcast_to(right[t : t + 1, :], (G, B)) for t in range(G)]
        for i in range(g + 1, B // G):
            a, b = rows[i]
            coef = outer[i - g - 1]
            for t in range(G):
                a = a - coef[t] * left_rows[t]
                b = b - coef[t] * right_rows[t]
            rows[i] = (a, b)
    u = jnp.concatenate(upper, axis=0)
    v = jnp.concatenate(inverse, axis=0)
    r = lax.broadcasted_iota(jnp.int32, (B, B), 0)
    c = lax.broadcasted_iota(jnp.int32, (B, B), 1)
    return jnp.where(c >= r, u, 0.0), v


MESH = pl.DeviceIdType.MESH


def padded(blocks, devices):
    return -(-blocks * B // (8 * devices)) * 8 * devices


def layout(count, dofs):
    half = count // 2
    return padded(half * (half + 1) // 2, 2 * dofs), padded(half * half, 4 * dofs)


def triangle(i, j, half):
    return (i * half - i * (i - 1) // 2 + (j - i)) * B


def block_rows(i, j, count, dofs):
    half = count // 2
    near, _ = layout(count, dofs)
    if j < half:
        return triangle(i, j, half)
    if i >= half:
        return near + triangle(i - half, j - half, half)
    return 2 * near + (i * half + j - half) * B


def radices_of(dofs):
    found = []
    left = dofs
    while left > 1:
        found.append(2 if not found else 4 if left % 4 == 0 else 2 if left % 2 == 0 else left)
        left //= found[-1]
    return found


def far_stages(dofs, first):
    d, s = lax.axis_index("dof"), lax.axis_index("snap")
    stages, stride = [], 1
    for n, radix in enumerate(radices_of(dofs)):
        digit = (d // stride) % radix
        if n >= first:
            stages.append(
                (
                    digit,
                    radix,
                    lambda j, g=digit, r=radix, t=stride: (d + t * ((g + j) % r - g), s),
                )
            )
        stride *= radix
    return stages


def gram_kernel(dofs, x_ref, active_ref, m_ref, g_ref, *scratch):
    slots, extra, near_ref, part1, part2, diag, total, own_sems, send_sems, recv_sems = scratch[:10]
    landing = list(scratch[10:])
    d, s = lax.axis_index("dof"), lax.axis_index("snap")
    core, y, x = s % 2, s // 2, d % 2
    rest = 1 - core
    rows, panel = slots.shape[1], slots.shape[2]
    width = m_ref.shape[1]
    count = width // B
    half = count // 2
    near = part1.shape[0]
    cross = part2.shape[0]
    beside, over, across = s + 1 - 2 * core, (s + 2) % 4, (s + 1 - 2 * core + 2) % 4
    pair = (core, 2, lambda j: (d, beside))
    dof_stages = far_stages(dofs, 0)
    stages1 = [pair] + dof_stages
    stages2 = [
        pair,
        (
            rest * x + core * y,
            2,
            lambda j: (d + rest * (1 - 2 * x), s + core * 2 * (1 - 2 * y)),
        ),
        (
            rest * y + core * x,
            2,
            lambda j: (d + core * (1 - 2 * x), s + rest * 2 * (1 - 2 * y)),
        ),
    ] + dof_stages[1:]

    greet = [(d, beside), (d, over), (d, across)]
    for _, radix, peer in dof_stages:
        greet += [peer(j) for j in range(1, radix)]
    barrier = pltpu.get_barrier_semaphore()
    for device in greet:
        pl.semaphore_signal(barrier, inc=1, device_id=device, device_id_type=MESH)
    pl.semaphore_wait(barrier, len(greet))

    used = []

    def send(src, dst, device):
        n = len(used)
        used.append(n)
        copy = pltpu.make_async_remote_copy(
            src_ref=src,
            dst_ref=dst,
            send_sem=send_sems.at[n],
            recv_sem=recv_sems.at[n],
            device_id=device,
            device_id_type=MESH,
        )
        copy.start()
        return copy

    def quarter(q):
        return x_ref.at[pl.ds(pl.multiple_of(q * rows, 16), rows), :]

    def span(offset, size):
        return pl.ds(pl.multiple_of(offset, 8), size)

    def scatter(stages, part, put):
        offset, length = 0, part.shape[0]
        spans = []
        for n, (digit, radix, peer) in enumerate(stages):
            size = length // radix
            arrive = landing.pop(0)
            copies = [
                send(
                    part.at[span(offset + ((digit + j) % radix) * size, size), :],
                    arrive.at[j - 1],
                    peer(j),
                )
                for j in range(1, radix)
            ]
            offset, length = offset + digit * size, size
            spans.append((offset, size))
            for copy in copies:
                copy.wait_recv()
            value = part[span(offset, size), :]
            for j in range(1, radix):
                value = value + arrive[j - 1]
            if n == len(stages) - 1:
                put(span(offset, size), value)
            else:
                part[span(offset, size), :] = value
            for copy in copies:
                copy.wait_send()
        return spans

    def gather(stages, spans, view):
        for n in reversed(range(len(stages))):
            _, radix, peer = stages[n]
            here = view(span(*spans[n]))
            copies = [send(here, here, peer(j)) for j in range(1, radix)]
            for copy in copies:
                copy.wait_recv()
            for copy in copies:
                copy.wait_send()

    pair_copies = [
        send(quarter(beside), slots.at[s], (d, beside)),
        send(quarter(across), extra.at[core], (d, beside)),
    ]
    far_copies = [
        send(quarter(over), slots.at[s], (d, over)),
        send(quarter(across), slots.at[s], (d, across)),
    ]
    own = [
        pltpu.make_async_copy(quarter(s), slots.at[s], own_sems.at[0]),
        pltpu.make_async_copy(quarter(over), extra.at[core], own_sems.at[1]),
    ]
    for copy in own:
        copy.start()
    for copy in own:
        copy.wait()
    for copy in pair_copies:
        copy.wait_recv()

    for i in range(2):
        columns = slice(i * panel, (i + 1) * panel)
        q = 2 * y + i
        keep = active_ref[0:1, pl.ds(pl.multiple_of(q * panel, panel), panel)]
        near_ref[:rows, columns] = (slots[q].astype(F32) * keep).astype(BF16)
        near_ref[rows:, columns] = (extra[i].astype(F32) * keep).astype(BF16)
    for i in range(half):
        strip = lax.dot_general(
            near_ref[:, i * B : (i + 1) * B],
            near_ref[:, i * B :],
            COL0,
            preferred_element_type=F32,
        )
        for j in range(i, half):
            first = triangle(i, j, half)
            part1[first : first + B, :] = strip[:, (j - i) * B : (j - i + 1) * B]
    end = half * (half + 1) // 2 * B
    if end < near:
        part1[end:, :] = jnp.zeros((near - end, B), F32)

    def put_diag(here, value):
        diag[y, here, :] = value

    spans = scatter(stages1, part1, put_diag)
    gather(stages1, spans, lambda here: diag.at[y, here, :])
    mine = span(core * (near // 2), near // 2)
    swap = send(diag.at[y, mine, :], diag.at[y, mine, :], (d, over))

    for copy in far_copies:
        copy.wait_recv()
    for i in range(4):
        columns = slice(i * panel, (i + 1) * panel)
        m_ref[:, columns] = (
            slots[i].astype(F32) * active_ref[0:1, columns]
        ).astype(BF16)
    for i in range(half):
        strip = lax.dot_general(
            m_ref[:, i * B : (i + 1) * B],
            m_ref[:, half * B :],
            COL0,
            preferred_element_type=F32,
        )
        for j in range(half):
            first = (i * half + j) * B
            part2[first : first + B, :] = strip[:, j * B : (j + 1) * B]
    end = half * half * B
    if end < cross:
        part2[end:, :] = jnp.zeros((cross - end, B), F32)

    def put_total(here, value):
        total[here, :] = value

    spans = scatter(stages2, part2, put_total)
    swap.wait_recv()
    other = diag.at[1 - y, mine, :]
    share = send(other, other, (d, beside))
    gather(stages2, spans, lambda here: total.at[here, :])
    share.wait_recv()
    g_ref[:near, :] = diag[0]
    g_ref[near : 2 * near, :] = diag[1]
    g_ref[2 * near :, :] = total[...]
    for copy in [*pair_copies, *far_copies, swap, share]:
        copy.wait_send()


def gram_of(snapshots, active, dofs, snaps):
    rows, panel = snapshots.shape[0] // snaps, snapshots.shape[1]
    width = panel * snaps
    near, cross = layout(width // B, dofs)
    far = radices_of(dofs)
    landing, copies = [], 6
    for radices, length in (([2] + far, near), ([2, 2] + far, cross)):
        for radix in radices:
            length //= radix
            landing.append(pltpu.VMEM((radix - 1, length, B), F32))
            copies += 2 * (radix - 1)
    return pl.pallas_call(
        functools.partial(gram_kernel, dofs),
        out_shape=(
            jax.ShapeDtypeStruct((rows, width), BF16),
            jax.ShapeDtypeStruct((2 * near + cross, B), F32),
        ),
        in_specs=[
            pl.BlockSpec(memory_space=pl.ANY),
            pl.BlockSpec(memory_space=pltpu.VMEM),
        ],
        out_specs=(pl.BlockSpec(memory_space=pltpu.VMEM),) * 2,
        scratch_shapes=[
            pltpu.VMEM((snaps, rows, panel), BF16),
            pltpu.VMEM((2, rows, panel), BF16),
            pltpu.VMEM((2 * rows, 2 * panel), BF16),
            pltpu.VMEM((near, B), F32),
            pltpu.VMEM((cross, B), F32),
            pltpu.VMEM((2, near, B), F32),
            pltpu.VMEM((cross, B), F32),
            pltpu.SemaphoreType.DMA((2,)),
            pltpu.SemaphoreType.DMA((copies,)),
            pltpu.SemaphoreType.DMA((copies,)),
            *landing,
        ],
        compiler_params=pltpu.CompilerParams(
            collective_id=0, has_side_effects=True, vmem_limit_bytes=VMEM_LIMIT
        ),
        name="gram",
    )(snapshots, active)


def shifted_block(g_ref, i, j, count, dofs, row_count):
    first = block_rows(i, j, count, dofs)
    block = g_ref[first : first + B, :] / F32(row_count)
    if i == j:
        r = lax.broadcasted_iota(jnp.int32, (B, B), 0)
        c = lax.broadcasted_iota(jnp.int32, (B, B), 1)
        block = block + jnp.where(r == c, 0.05, 0.0).astype(F32)
    return block


def cholesky_kernel(dofs, row_count, g_ref, r_ref, left_ref, right_ref):
    width = r_ref.shape[0]
    count = width // B
    for i in range(count):
        r_ref[i * B : (i + 1) * B, :] = jnp.zeros((B, width), F32)
        for j in range(i, count):
            r_ref[i * B : (i + 1) * B, j * B : (j + 1) * B] = shifted_block(
                g_ref, i, j, count, dofs, row_count
            )

    @pl.loop(0, count)
    def panel(k):
        here = pl.ds(pl.multiple_of(k * B, B), B)
        u, v = factor_block(r_ref[here, here])
        row = dot6(v, r_ref[here, :], ROWCOL)
        col = lax.broadcasted_iota(jnp.int32, (B, width), 1)
        row = jnp.where(col >= (k + 1) * B, row, 0.0)
        r_ref[here, :] = row
        r_ref[here, here] = u
        hi, mid, low = split3(row)
        left_ref[...] = jnp.concatenate([hi, mid, hi, low, mid, hi], axis=0)
        right_ref[...] = jnp.concatenate([hi, hi, mid, hi, mid, low], axis=0)

        @pl.loop(k + 1, count)
        def update(i):
            there = pl.ds(pl.multiple_of(i * B, B), B)
            r_ref[there, :] = r_ref[there, :] - lax.dot_general(
                left_ref[:, there], right_ref[...], COL0, preferred_element_type=F32
            )


def cholesky(packed, width, dofs, row_count):
    return pl.pallas_call(
        functools.partial(cholesky_kernel, dofs, row_count),
        out_shape=jax.ShapeDtypeStruct((width, width), F32),
        in_specs=[pl.BlockSpec(memory_space=pltpu.VMEM)],
        out_specs=pl.BlockSpec(memory_space=pltpu.VMEM),
        scratch_shapes=[
            pltpu.VMEM((6 * B, width), BF16),
            pltpu.VMEM((6 * B, width), BF16),
        ],
        compiler_params=pltpu.CompilerParams(vmem_limit_bytes=VMEM_LIMIT),
        name="cholesky",
    )(packed)


def iterate_kernel(dofs, row_count, g_ref, x_ref, full_ref, hi_ref, mid_ref, low_ref):
    width, modes = x_ref.shape
    o_ref = full_ref.at[:, :modes]
    full_ref[:, modes:] = jnp.zeros((width, width - modes), F32)
    count = width // B
    for i in range(count):
        for j in range(i, count):
            block = shifted_block(g_ref, i, j, count, dofs, row_count)
            a, b = slice(i * B, (i + 1) * B), slice(j * B, (j + 1) * B)
            hi_ref[a, b], mid_ref[a, b], low_ref[a, b] = split3(block)
            if i < j:
                hi_ref[b, a], mid_ref[b, a], low_ref[b, a] = split3(block.T)
    o_ref[...] = x_ref[...]

    @pl.loop(0, ITERS)
    def sweep(_):
        x1, x2, x3 = split3(o_ref[...])
        first = lax.dot_general(
            hi_ref[...],
            jnp.concatenate([x1, x2, x3], axis=1),
            ROWCOL,
            preferred_element_type=F32,
        )
        second = lax.dot_general(
            mid_ref[...],
            jnp.concatenate([x1, x2], axis=1),
            ROWCOL,
            preferred_element_type=F32,
        )
        third = lax.dot_general(low_ref[...], x1, ROWCOL, preferred_element_type=F32)
        image = (
            (third + second[:, modes:] + first[:, 2 * modes :])
            + (first[:, modes : 2 * modes] + second[:, :modes])
            + first[:, :modes]
        )
        correlation = dot6(image, image, COL0)
        _, v = factor_block(correlation)
        o_ref[...] = dot6(image, v, COLCOL)


def iterate(packed, start_block, dofs, row_count):
    width, modes = start_block.shape
    return pl.pallas_call(
        functools.partial(iterate_kernel, dofs, row_count),
        out_shape=jax.ShapeDtypeStruct((width, width), F32),
        in_specs=[pl.BlockSpec(memory_space=pltpu.VMEM)] * 2,
        out_specs=pl.BlockSpec(memory_space=pltpu.VMEM),
        scratch_shapes=[pltpu.VMEM((width, width), BF16)] * 3,
        compiler_params=pltpu.CompilerParams(vmem_limit_bytes=VMEM_LIMIT),
        name="iterate",
    )(packed, start_block)


def finish_kernel(first_ref, mine_ref, got_ref, m_ref, o_ref, r_ref, block_ref, sems):
    modes = o_ref.shape[1]
    first = first_ref[0] == 1

    def finish(r_source, b_source):
        factor = pltpu.make_async_copy(r_source, r_ref, sems.at[0])
        block = pltpu.make_async_copy(b_source.at[:, :modes], block_ref, sems.at[1])
        block.start()
        factor.start()
        block.wait()
        b1, b2, b3 = split3(block_ref[...])
        parts = lax.dot_general(
            m_ref[...],
            jnp.concatenate([b1, b2, b3], axis=1),
            ROWCOL,
            preferred_element_type=F32,
        )
        o_ref[...] = (parts[:, 2 * modes :] + parts[:, modes : 2 * modes]) + parts[:, :modes]
        factor.wait()

    @pl.when(first)
    def _():
        finish(mine_ref, got_ref)

    @pl.when(jnp.logical_not(first))
    def _():
        finish(got_ref, mine_ref)


def finish_of(first, mine, got, masked, modes):
    return pl.pallas_call(
        finish_kernel,
        out_shape=(
            jax.ShapeDtypeStruct((masked.shape[0], modes), F32),
            jax.ShapeDtypeStruct(mine.shape, F32),
        ),
        in_specs=[
            pl.BlockSpec(memory_space=pltpu.SMEM),
            pl.BlockSpec(memory_space=pl.ANY),
            pl.BlockSpec(memory_space=pl.ANY),
            pl.BlockSpec(memory_space=pltpu.VMEM),
        ],
        out_specs=(
            pl.BlockSpec(memory_space=pltpu.VMEM),
            pl.BlockSpec(memory_space=pl.ANY),
        ),
        scratch_shapes=[
            pltpu.VMEM((mine.shape[0], modes), F32),
            pltpu.SemaphoreType.DMA((2,)),
        ],
        compiler_params=pltpu.CompilerParams(vmem_limit_bytes=VMEM_LIMIT // 2),
        name="finish",
    )(first, mine, got, masked)


def active_columns(lengths, width):
    columns = jnp.arange(width, dtype=jnp.int32)
    lookup = (columns // STEPS)[:, None] == jnp.arange(PASSES, dtype=jnp.int32)[None, :]
    col_length = jnp.sum(jnp.where(lookup, lengths[None, :], 0), axis=1)
    return columns % STEPS < col_length


def body(snapshots, lengths, start_block):
    dofs, snap = lax.axis_size("dof"), lax.axis_size("snap")
    width = start_block.shape[0]
    row_count = snapshots.shape[0] * dofs
    active = jnp.broadcast_to(active_columns(lengths, width).astype(F32)[None, :], (8, width))
    masked, packed = gram_of(snapshots, active, dofs, snap)
    first = lax.axis_index("snap") % 2 == 0
    mine = lax.cond(
        first,
        lambda: cholesky(packed, width, dofs, row_count),
        lambda: iterate(packed, start_block, dofs, row_count),
    )
    got = lax.ppermute(mine, "snap", [(i, i + 1 - 2 * (i % 2)) for i in range(snap)])
    return finish_of(first.astype(jnp.int32).reshape(1), mine, got, masked, start_block.shape[1])


def solution(mesh):
    placed = (P("dof", "snap"), P(), P())
    return jax.shard_map(
        body, mesh=mesh, in_specs=placed, out_specs=(P(("dof", "snap"), None), P()), check_vma=False
    )
```
